32 devices in a mesh: node: 4 (over y, core), hst: 8 (over z, x).
Axes of the slice: x: 2, y: 2, z: 4, core: 2. Of those that a mesh axis runs over, the one named last changes fastest.
Arguments:
- hidden: bfloat16 [8, 4096, 640], P('hst', 'node'), may hold values from -6 to 6
- cotangent: bfloat16 [8, 4096, 4608], P('hst', 'node'), may hold values from -12 to 12
- anchor: float32 [8, 640, 4608], P('hst', 'node'), may hold values from -0.25 to 0.25
- momentum: float32 [8, 640, 4608], P('hst', 'node'), may hold values from -0.6 to 0.6
- round_mask: int32 [1], replicated, may hold values from 1 to 7
Outputs:
- weights_out: bfloat16 [8, 640, 4608], P('hst')
- momentum_out: float32 [8, 640, 4608], P('hst', 'node')
The draws below stay inside these ranges and needn't reach their ends.
Inputs may be any that keep to these rules, and one draw needn't show every extreme that they name: round_mask is the same for all hosts; host i averages with the hosts i XOR s for every s whose bits lie within round_mask.
All inputs are finite; a program needn't handle non-finite values.
Results may differ from the reference program's by a relative error of at most 0.009.
Values may be sent and summed in bfloat16 or wider, within the bound.
No kernel may reach another device: no remote copies, remote signals or barrier semaphores. Data moves between devices by JAX's collectives and lax.ppermute only.
A program may use at most 256 MiB of HBM per device.

```python
import jax
import jax.numpy as jnp
from jax import lax

D = 4608
H = 640
TOK_DEV = 1024
NODE_TOK = 4096
N_NODE = 4
N_HST = 8


def steps_of(rng, shape, shards, smallest, high):
    level, own = 1.0, jax.random.fold_in(rng, 6)
    for axis_at, shards_of in shards:
        steps = jnp.exp(jax.random.uniform(jax.random.fold_in(own, axis_at), (shards_of,), jnp.float32, smallest / len(shards), high / len(shards)))
        level = level * jnp.repeat(steps, shape[axis_at] // shards_of).reshape([-1 if axis == axis_at else 1 for axis in range(len(shape))])
    return level


def gaussian(stream_key, dims, width, reach, pieces=(), kind=jnp.bfloat16):
    factor_of = steps_of(stream_key, dims, pieces, -0.22, 0.18) if pieces else 1.0
    result = jax.random.normal(stream_key, dims, jnp.float32) * width * factor_of
    return jnp.minimum(jnp.maximum(result, -reach), reach).astype(kind)


def setup_inputs(seed: int = 0) -> dict:
    seeds = jax.random.split(jax.random.key(seed), 6)
    hidden = gaussian(seeds[0], (N_HST, NODE_TOK, H), 1.0, 6.0, ((0, 8), (1, 4)))
    cotangent = gaussian(seeds[1], (N_HST, NODE_TOK, D), 2.0, 12.0, ((0, 8), (1, 4)))
    anchor = gaussian(seeds[2], (N_HST, H, D), H ** -0.5, 0.25, ((0, 8), (1, 4)), jnp.float32)
    momentum = gaussian(seeds[3], (N_HST, H, D), 0.1, 0.6, ((0, 8), (1, 4)), jnp.float32)
    round_mask = jax.random.randint(seeds[4], (1,), 1, N_HST).astype(jnp.int32)
    return {"hidden": hidden, "cotangent": cotangent, "anchor": anchor, "momentum": momentum, "round_mask": round_mask}


base_rate = 0.5
slow_rate = 1.0
slow_beta = 0.7

def host_grad(inputs_pair):
    activations, cotangents = inputs_pair
    activations = activations.reshape(N_NODE, TOK_DEV, H)
    cotangents = cotangents.reshape(N_NODE, TOK_DEV, D)
    summed = jnp.zeros((H, D), jnp.float32)
    for device in range(N_NODE):
        product = jnp.dot(activations[device].T, cotangents[device], preferred_element_type=jnp.float32)
        product = product * (1.0 / (TOK_DEV * N_NODE))
        rounded = lax.optimization_barrier(product.astype(jnp.bfloat16))
        summed = summed + rounded.astype(jnp.float32)
    return summed

def reference(hidden, cotangent, anchor, momentum, round_mask):
    grads = lax.map(host_grad, (hidden, cotangent))
    stepped = anchor - base_rate * grads
    host_ids = jnp.arange(N_HST, dtype=jnp.int32)
    free_bits = jnp.bitwise_xor(round_mask[0], jnp.int32(N_HST - 1))
    mixing = (jnp.bitwise_and(jnp.bitwise_xor(host_ids[:, None], host_ids[None, :]), free_bits) == 0).astype(jnp.float32)
    mixing = mixing / lax.optimization_barrier(jnp.sum(mixing, axis=1, keepdims=True))
    averaged = jnp.tensordot(mixing, stepped, axes=1, precision=lax.Precision.HIGHEST)
    momentum_out = slow_beta * momentum + (anchor - averaged) / base_rate
    updated = anchor - slow_rate * base_rate * momentum_out
    return (updated.astype(jnp.bfloat16), momentum_out)
```

```python
import jax
import jax.numpy as jnp
from jax import lax
from jax.sharding import PartitionSpec as P

base_rate = 0.5
slow_rate = 1.0
slow_beta = 0.7
chunk_count = 2


def swapped(block, axis, bit):
    count = lax.axis_size(axis)
    return lax.ppermute(block, axis, [(i, i ^ (1 << bit)) for i in range(count)])


def pick(flag, pair):
    return jnp.where(flag == 1, pair[1], pair[0])


def half_of(index, bit):
    return jnp.bitwise_and(jnp.right_shift(index, bit), 1)


def node_sum(parts, node, bits):
    for bit in bits:
        mine = half_of(node, bit)
        low, high = parts[0::2], parts[1::2]
        send = [jnp.where(mine == 1, a, b).astype(jnp.bfloat16) for a, b in zip(low, high)]
        keep = [jnp.where(mine == 1, b, a) for a, b in zip(low, high)]
        got = swapped(jnp.stack(send), "node", bit)
        parts = [k + g.astype(jnp.float32) for k, g in zip(keep, got)]
    return parts[0]


def host_mean(block, host, order):
    halved = []
    count = 1
    rows = block.shape[0]
    for place, bit in enumerate(order):
        count *= 2
        if place < len(order) - 1 and rows % 16 == 0 and len(halved) < 2:
            rows //= 2
            mine = half_of(host, bit)
            low, high = block[:rows], block[rows:]
            got = swapped(pick(mine, (high, low)).astype(jnp.bfloat16), "hst", bit)
            block = pick(mine, (low, high)) + got.astype(jnp.float32)
            halved.append(bit)
        else:
            block = block + swapped(block.astype(jnp.bfloat16), "hst", bit).astype(jnp.float32)
    block = block * (1.0 / count)
    for bit in reversed(halved):
        mine = half_of(host, bit)
        got = swapped(block.astype(jnp.bfloat16), "hst", bit).astype(jnp.float32)
        block = jnp.concatenate([pick(mine, (block, got)), pick(mine, (got, block))], axis=0)
    return block


def update(orders, hidden, cotangent, anchor, momentum):
    tokens, width = cotangent.shape
    node_count = lax.axis_size("node")
    node_bits = range(node_count.bit_length() - 1)
    node, host = lax.axis_index("node"), lax.axis_index("hst")
    rows = anchor.shape[0]
    scale = 1.0 / (tokens * node_count)
    part = width // chunk_count
    weights = jnp.zeros((rows * node_count, width), jnp.bfloat16)
    momentum_parts = []
    for chunk in range(chunk_count):
        columns = slice(chunk * part, (chunk + 1) * part)
        product = lax.dot_general(
            hidden, cotangent[:, columns], (((0,), (0,)), ((), ())), preferred_element_type=jnp.float32
        ) * scale
        gradient = node_sum(list(product.reshape(node_count, rows, part)), node, node_bits)
        stepped = anchor[:, columns] - base_rate * gradient
        averaged = host_mean(stepped, host, orders[chunk % len(orders)])
        momentum_new = slow_beta * momentum[:, columns] + (anchor[:, columns] - averaged) / base_rate
        momentum_parts.append(momentum_new)
        updated = (anchor[:, columns] - slow_rate * base_rate * momentum_new).astype(jnp.bfloat16)
        have = [(node, updated)]
        for bit in reversed(node_bits):
            have += [(place ^ (1 << bit), swapped(block, "node", bit)) for place, block in have]
        for place, block in have:
            weights = lax.dynamic_update_slice(weights, block, (place * rows, chunk * part))
    return weights, jnp.concatenate(momentum_parts, axis=1)


def local(hidden, cotangent, anchor, momentum, round_mask):
    host_count = lax.axis_size("hst")
    branches = []
    for mask in range(1, host_count):
        bits = [b for b in range(host_count.bit_length() - 1) if mask >> b & 1]
        orders = [bits, bits[:-1][::-1] + bits[-1:]]
        branches.append(lambda *arrays, orders=orders: update(orders, *arrays))
    weights, momentum_new = lax.switch(
        round_mask[0] - 1, branches, hidden[0], cotangent[0], anchor[0], momentum[0]
    )
    return (weights[None], momentum_new[None])


def solution(mesh):
    placed = (
        P("hst", "node", None),
        P("hst", "node", None),
        P("hst", "node", None),
        P("hst", "node", None),
        P(),
    )
    return jax.shard_map(
        local,
        mesh=mesh,
        in_specs=placed,
        out_specs=(P("hst", None, None), P("hst", "node", None)),
        check_vma=False,
    )
```

```python
import jax
import jax.numpy as jnp
from jax import lax
from jax.experimental import pallas as pl
from jax.experimental.pallas import tpu as pltpu
from jax.sharding import PartitionSpec as P

base_rate = 0.5
slow_rate = 1.0
slow_beta = 0.7
chunk_count = 2


def swapped(block, axis, bit):
    count = lax.axis_size(axis)
    return lax.ppermute(block, axis, [(i, i ^ (1 << bit)) for i in range(count)])


def bit_of(index, bit):
    return jnp.bitwise_and(jnp.right_shift(index, bit), 1)


def wide(block):
    return block.astype(jnp.float32)


def narrow(block):
    return block.astype(jnp.bfloat16)


def pick(flag, low, high):
    return jnp.where(flag == 1, high, low)


def chunk_steps(order, hidden, cotangent, anchor, momentum, scale):
    rows, part = anchor.shape
    node, host = lax.axis_index("node"), lax.axis_index("hst")
    node_count = lax.axis_size("node")
    node_bits = list(range(node_count.bit_length() - 1))
    product = lax.dot_general(hidden, cotangent, (((0,), (0,)), ((), ())), preferred_element_type=jnp.float32)
    parts = narrow(product * scale).reshape(node_count, rows, part)
    for bit in node_bits:
        pairs = parts.reshape(-1, 2, rows, part)
        mine = bit_of(node, bit)
        send = narrow(lax.dynamic_index_in_dim(pairs, 1 - mine, 1, keepdims=False))
        keep = lax.dynamic_index_in_dim(pairs, mine, 1, keepdims=False)
        (got,) = yield [(send, "node", bit)], None, None
        parts = wide(keep) + wide(got)
    block = anchor - base_rate * parts[0]
    halved = []
    count = 1
    for place, bit in enumerate(order):
        count *= 2
        if place < len(order) - 1 and rows % 16 == 0 and len(halved) < 2:
            rows //= 2
            mine = bit_of(host, bit)
            low, high = block[:rows], block[rows:]
            (got,) = yield [(narrow(pick(mine, high, low)), "hst", bit)], None, None
            block = pick(mine, low, high) + wide(got)
            halved.append(bit)
        else:
            (got,) = yield [(narrow(block), "hst", bit)], None, None
            block = block + wide(got)
    block = block * (1.0 / count)
    for bit in reversed(halved):
        mine = bit_of(host, bit)
        (got,) = yield [(narrow(block), "hst", bit)], None, None
        block = jnp.concatenate([pick(mine, block, wide(got)), pick(mine, wide(got), block)], axis=0)
    momentum_new = slow_beta * momentum + (anchor - block) / base_rate
    updated = narrow(anchor - slow_rate * base_rate * momentum_new)
    flips, blocks = [0], [updated]
    fresh, fresh_flips = blocks, flips
    for bit in reversed(node_bits):
        gots = yield [(b, "node", bit) for b in blocks], fresh, fresh_flips
        fresh, fresh_flips = gots, [f ^ (1 << bit) for f in flips]
        flips, blocks = flips + fresh_flips, blocks + fresh
    return momentum_new, fresh, fresh_flips


def put_blocks(weights, blocks, flips, column, shape):
    part = blocks[0].shape[1]

    def kernel(*refs):
        out, sems = refs[-2:]
        node = lax.axis_index("node")
        copies = [
            pltpu.make_async_copy(
                refs[i], out.at[jnp.bitwise_xor(node, flip), :, pl.ds(column, part)], sems.at[i]
            )
            for i, flip in enumerate(flips)
        ]
        for copy in copies:
            copy.start()
        for copy in copies:
            copy.wait()

    held = [] if weights is None else [weights]
    return pl.pallas_call(
        kernel,
        out_shape=jax.ShapeDtypeStruct(shape, jnp.bfloat16),
        in_specs=[pl.BlockSpec(memory_space=pl.ANY)] * len(blocks)
        + [pl.BlockSpec(memory_space=pltpu.HBM)] * len(held),
        out_specs=pl.BlockSpec(memory_space=pltpu.HBM),
        scratch_shapes=[pltpu.SemaphoreType.DMA((len(blocks),))],
        input_output_aliases={len(blocks): 0} if held else {},
        cost_estimate=pl.CostEstimate(flops=0, bytes_accessed=2 * len(blocks) * blocks[0].size * 2, transcendentals=0),
    )(*blocks, *held)


def link_time(send, axis, bit):
    megabytes = send.size * 2 / 1e6
    if axis == "node" and bit == 0:
        return megabytes / 0.35, "core"
    if axis == "node":
        return 2 * megabytes / 0.094, "y"
    return 2 * megabytes / 0.094 * (2 if bit >= 2 else 1), "x" if bit == 0 else "z"


def update(orders, hidden, cotangent, anchor, momentum):
    tokens, width = cotangent.shape
    rows = anchor.shape[0]
    node_count = lax.axis_size("node")
    scale = 1.0 / (tokens * node_count)
    part = width // chunk_count
    columns = [slice(k * part, (k + 1) * part) for k in range(chunk_count)]
    chunks = [
        chunk_steps(orders[k % len(orders)], hidden, cotangent[:, c], anchor[:, c], momentum[:, c], scale)
        for k, c in enumerate(columns)
    ]
    weights = None
    momentum_parts = [None] * chunk_count
    arrived = [None] * chunk_count
    last = None
    ready = {0: 0.0}
    now, link_free = 0.0, {}
    while ready:
        k = min(ready, key=lambda c: (ready[c], c))
        now = max(now, ready.pop(k)) + (10.0 / chunk_count if arrived[k] is None else 1.5)
        first = arrived[k] is None
        if not first and last is not None:
            arrived[k], last = lax.optimization_barrier((arrived[k], last))
        try:
            blocks = None
            sends, blocks, flips = chunks[k].send(arrived[k])
            sends = [(lax.optimization_barrier(a), *how) for a, *how in sends]
            last = sends[0][0]
            arrived[k] = [swapped(*s) for s in sends]
            ends = []
            for s in sends:
                took, link = link_time(*s)
                now += 1.5
                link_free[link] = max(now, link_free.get(link, 0.0)) + took
                ends.append(link_free[link])
            ready[k] = max(ends)
        except StopIteration as end:
            momentum_parts[k], blocks, flips = end.value
        if blocks:
            weights = put_blocks(weights, blocks, flips, k * part, (node_count, rows, width))
        if first and k + 1 < chunk_count:
            ready[k + 1] = now
    return weights.reshape(-1, width), jnp.concatenate(momentum_parts, axis=1)


def local(hidden, cotangent, anchor, momentum, round_mask):
    host_count = lax.axis_size("hst")
    branches = []
    for mask in range(1, host_count):
        bits = [b for b in range(host_count.bit_length() - 1) if mask >> b & 1]
        orders = [bits, bits[:-1][::-1] + bits[-1:]]
        branches.append(lambda *arrays, orders=orders: update(orders, *arrays))
    weights, momentum_new = lax.switch(
        round_mask[0] - 1, branches, hidden[0], cotangent[0], anchor[0], momentum[0]
    )
    return (weights[None], momentum_new[None])


def solution(mesh):
    placed = (
        P("hst", "node", None),
        P("hst", "node", None),
        P("hst", "node", None),
        P("hst", "node", None),
        P(),
    )
    return jax.shard_map(
        local,
        mesh=mesh,
        in_specs=placed,
        out_specs=(P("hst", None, None), P("hst", "node", None)),
        check_vma=False,
    )
```

```python
import jax
import jax.numpy as jnp
from jax import lax
from jax.sharding import PartitionSpec as P

base_rate = 0.5
slow_rate = 1.0
slow_beta = 0.7
chunk_count = 2


def swapped(block, axis, bit):
    count = lax.axis_size(axis)
    return lax.ppermute(block, axis, [(i, i ^ (1 << bit)) for i in range(count)])


def bit_of(index, bit):
    return jnp.bitwise_and(jnp.right_shift(index, bit), 1)


def wide(block):
    return block.astype(jnp.float32)


def narrow(block):
    return block.astype(jnp.bfloat16)


def pick(flag, low, high):
    return jnp.where(flag == 1, high, low)


def chunk_steps(order, hidden, cotangent, anchor, momentum, scale):
    rows, part = anchor.shape
    node, host = lax.axis_index("node"), lax.axis_index("hst")
    node_count = lax.axis_size("node")
    node_bits = list(range(node_count.bit_length() - 1))
    product = lax.dot_general(hidden, cotangent, (((0,), (0,)), ((), ())), preferred_element_type=jnp.float32)
    parts = narrow(product * scale).reshape(node_count, rows, part)
    for bit in node_bits:
        pairs = parts.reshape(-1, 2, rows, part)
        mine = bit_of(node, bit)
        send = narrow(lax.dynamic_index_in_dim(pairs, 1 - mine, 1, keepdims=False))
        keep = lax.dynamic_index_in_dim(pairs, mine, 1, keepdims=False)
        (got,) = yield [(send, "node", bit)], None, None
        parts = wide(keep) + wide(got)
    block = anchor - base_rate * parts[0]
    halved = []
    count = 1
    for place, bit in enumerate(order):
        count *= 2
        if place < len(order) - 1 and rows % 16 == 0 and len(halved) < 2:
            rows //= 2
            mine = bit_of(host, bit)
            low, high = block[:rows], block[rows:]
            (got,) = yield [(narrow(pick(mine, high, low)), "hst", bit)], None, None
            block = pick(mine, low, high) + wide(got)
            halved.append(bit)
        else:
            (got,) = yield [(narrow(block), "hst", bit)], None, None
            block = block + wide(got)
    block = block * (1.0 / count)
    for bit in reversed(halved):
        mine = bit_of(host, bit)
        (got,) = yield [(narrow(block), "hst", bit)], None, None
        block = jnp.concatenate([pick(mine, block, wide(got)), pick(mine, wide(got), block)], axis=0)
    momentum_new = slow_beta * momentum + (anchor - block) / base_rate
    updated = narrow(anchor - slow_rate * base_rate * momentum_new)
    flips, blocks = [0], [updated]
    fresh, fresh_flips = blocks, flips
    for bit in reversed(node_bits):
        gots = yield [(b, "node", bit) for b in blocks], fresh, fresh_flips
        fresh, fresh_flips = gots, [f ^ (1 << bit) for f in flips]
        flips, blocks = flips + fresh_flips, blocks + fresh
    return momentum_new, fresh, fresh_flips


def update(orders, hidden, cotangent, anchor, momentum):
    tokens, width = cotangent.shape
    rows = anchor.shape[0]
    node_count = lax.axis_size("node")
    node = lax.axis_index("node")
    scale = 1.0 / (tokens * node_count)
    part = width // chunk_count
    columns = [slice(k * part, (k + 1) * part) for k in range(chunk_count)]
    chunks = [
        chunk_steps(orders[k % len(orders)], hidden, cotangent[:, c], anchor[:, c], momentum[:, c], scale)
        for k, c in enumerate(columns)
    ]
    weights = jnp.zeros((node_count, rows, width), jnp.bfloat16)
    momentum_parts = [None] * chunk_count
    arrived = [None] * chunk_count
    steps = [0] * chunk_count
    last = None
    waiting = list(range(min(2, chunk_count)))
    fresh_chunk = len(waiting)
    while waiting:
        k = waiting.pop(0)
        if arrived[k] is not None and last is not None:
            arrived[k], last = lax.optimization_barrier((arrived[k], last))
        try:
            blocks = None
            sends, blocks, flips = chunks[k].send(arrived[k])
            sends = [(lax.optimization_barrier(a), *how) for a, *how in sends]
            last = [a for a, *_ in sends]
            arrived[k] = [swapped(*s) for s in sends]
            steps[k] += 1
            waiting.append(k)
            if steps[k] == 2 and fresh_chunk < chunk_count:
                waiting.insert(0, fresh_chunk)
                fresh_chunk += 1
        except StopIteration as end:
            momentum_parts[k], blocks, flips = end.value
        for block, flip in zip(blocks or [], flips or []):
            weights = lax.dynamic_update_slice(
                weights, block[None], (jnp.bitwise_xor(node, flip), 0, k * part)
            )
    return weights.reshape(-1, width), jnp.concatenate(momentum_parts, axis=1)


def local(hidden, cotangent, anchor, momentum, round_mask):
    host_count = lax.axis_size("hst")
    branches = []
    for mask in range(1, host_count):
        bits = [b for b in range(host_count.bit_length() - 1) if mask >> b & 1]
        orders = [bits, bits[:-1][::-1] + bits[-1:]]
        branches.append(lambda *arrays, orders=orders: update(orders, *arrays))
    weights, momentum_new = lax.switch(
        round_mask[0] - 1, branches, hidden[0], cotangent[0], anchor[0], momentum[0]
    )
    return (weights[None], momentum_new[None])


def solution(mesh):
    placed = (
        P("hst", "node", None),
        P("hst", "node", None),
        P("hst", "node", None),
        P("hst", "node", None),
        P(),
    )
    return jax.shard_map(
        local,
        mesh=mesh,
        in_specs=placed,
        out_specs=(P("hst", None, None), P("hst", "node", None)),
        check_vma=False,
    )
```

```python
import jax
import jax.numpy as jnp
from jax import lax
from jax.experimental import pallas as pl
from jax.experimental.pallas import tpu as pltpu
from jax.sharding import PartitionSpec as P

base_rate = 0.5
slow_rate = 1.0
slow_beta = 0.7
chunk_shares = (1, 1, 1, 1)


def swapped(block, axis, bit):
    count = lax.axis_size(axis)
    return lax.ppermute(block, axis, [(i, i ^ (1 << bit)) for i in range(count)])


def bit_of(index, bit):
    return jnp.bitwise_and(jnp.right_shift(index, bit), 1)


def wide(block):
    return block.astype(jnp.float32)


def narrow(block):
    return block.astype(jnp.bfloat16)


def pick(flag, low, high):
    return jnp.where(flag == 1, high, low)


def chosen(blocks, index):
    return lax.dynamic_index_in_dim(blocks, index, 1, keepdims=False)


def partial_product(hidden, cotangent, start, part, scale, turned):
    node_count = lax.axis_size("node")
    tokens = cotangent.shape[0]
    height = hidden.shape[0 if turned else 1]
    rows = height // node_count
    tile = max(t for t in range(128, 513, 128) if part % t == 0 and start % t == 0)

    def kernel(hidden_ref, cotangent_ref, send_ref, keep_ref, *rest):
        core = jnp.bitwise_and(lax.axis_index("node"), 1)
        if turned:
            left = hidden_ref
        else:
            left = rest[0]

            @pl.when(pl.program_id(0) == 0)
            def _():
                left[...] = hidden_ref[...].T

        product = jnp.dot(left[...], cotangent_ref[...], preferred_element_type=jnp.float32)
        product = narrow(product * scale)
        for pair in range(node_count // 2):
            low = product[2 * pair * rows : (2 * pair + 1) * rows]
            high = product[(2 * pair + 1) * rows : (2 * pair + 2) * rows]
            send_ref[pair] = jnp.where(core == 1, low, high)
            keep_ref[pair] = jnp.where(core == 1, high, low)

    half = jax.ShapeDtypeStruct((node_count // 2, rows, part), jnp.bfloat16)
    block = pl.BlockSpec((node_count // 2, rows, tile), lambda j: (0, 0, j))
    extra = [] if turned else [jax.ShapeDtypeStruct((height, tokens), jnp.bfloat16)]
    return pl.pallas_call(
        kernel,
        grid=(part // tile,),
        out_shape=[half, half] + extra,
        in_specs=[
            pl.BlockSpec(hidden.shape, lambda j: (0, 0)),
            pl.BlockSpec((tokens, tile), lambda j: (0, start // tile + j)),
        ],
        out_specs=[block, block] + [pl.BlockSpec((height, tokens), lambda j: (0, 0)) for _ in extra],
        compiler_params=pltpu.CompilerParams(vmem_limit_bytes=24 * 2**20),
        cost_estimate=pl.CostEstimate(
            flops=2 * tokens * height * part,
            bytes_accessed=2 * (tokens * height + tokens * part + height * part),
            transcendentals=0,
        ),
    )(hidden, cotangent)


def chunk_steps(plan, send, keep, anchor, momentum):
    node, host = lax.axis_index("node"), lax.axis_index("hst")
    node_bits = list(range(lax.axis_size("node").bit_length() - 1))
    (got,) = yield [(send, "node", 0)], []
    terms = [keep, got]
    for bit in node_bits[1:]:
        mine = bit_of(node, bit)
        pairs = [t.reshape(-1, 2, *t.shape[1:]) for t in terms]
        send = narrow(sum(wide(chosen(p, 1 - mine)) for p in pairs))
        (got,) = yield [(send, "node", bit)], []
        terms = [chosen(p, mine) for p in pairs] + [got]
    block = anchor - base_rate * sum(wide(t[0]) for t in terms)
    count = 1
    halved = []
    for bit, by_halves in plan:
        count *= 2
        if by_halves:
            rows = block.shape[0] // 2
            mine = bit_of(host, bit)
            low, high = block[:rows], block[rows:]
            (got,) = yield [(narrow(pick(mine, high, low)), "hst", bit)], []
            block = pick(mine, low, high) + wide(got)
            halved.append(bit)
        else:
            (got,) = yield [(narrow(block), "hst", bit)], []
            block = block + wide(got)
    block = block * (1.0 / count)
    for bit in reversed(halved):
        mine = bit_of(host, bit)
        (got,) = yield [(narrow(block), "hst", bit)], []
        block = jnp.concatenate([pick(mine, block, wide(got)), pick(mine, wide(got), block)], axis=0)
    updated = narrow(
        (1.0 - slow_rate) * anchor + slow_rate * block - slow_rate * base_rate * slow_beta * momentum
    )
    momentum_new = slow_beta * momentum + (anchor - block) / base_rate
    fresh = [(updated, 0, len(node_bits))]
    while True:
        sends = [(b, "node", bit) for b, _, top in fresh for bit in reversed(range(top))]
        if not sends:
            return momentum_new, fresh
        routes = [(flip | 1 << bit, bit) for _, flip, top in fresh for bit in reversed(range(top))]
        gots = yield sends, fresh
        fresh = [(g, flip, bit) for g, (flip, bit) in zip(gots, routes)]


def update(plan, hidden, cotangent, anchor, momentum):
    tokens, width = cotangent.shape
    rows = anchor.shape[0]
    node_count = lax.axis_size("node")
    node = lax.axis_index("node")
    scale = 1.0 / (tokens * node_count)
    chunk_count = len(chunk_shares)
    unit = width // sum(chunk_shares)
    bounds = [unit * sum(chunk_shares[:k]) for k in range(chunk_count + 1)]
    weights = None
    chunks = []
    momentum_parts = [None] * chunk_count
    arrived = []
    steps = []
    last = None
    left = hidden

    def begin(k):
        nonlocal left, last
        if last is not None:
            (left,), last = lax.optimization_barrier(((left,), last))
        columns = slice(bounds[k], bounds[k + 1])
        send, keep, *rest = partial_product(
            left, cotangent, bounds[k], bounds[k + 1] - bounds[k], scale, turned=k > 0
        )
        left = rest[0] if rest else left
        chunks.append(chunk_steps(plan, send, keep, anchor[:, columns], momentum[:, columns]))
        arrived.append(None)
        steps.append(0)

    waiting = []
    for k in range(min(2, chunk_count)):
        waiting.append(k)
    while waiting:
        k = waiting.pop(0)
        if k == len(chunks):
            begin(k)
        else:
            held = [] if weights is None else [weights]
            arrived[k], last, held = lax.optimization_barrier((arrived[k], last, held))
            weights = held[0] if held else jnp.zeros((node_count, rows, width), jnp.bfloat16)
        try:
            sends, blocks = chunks[k].send(arrived[k])
            sends = [(lax.optimization_barrier(a), *how) for a, *how in sends]
            last = [a for a, *_ in sends]
            arrived[k] = [swapped(*s) for s in sends]
            steps[k] += 1
            waiting.append(k)
            if steps[k] == 2 and len(chunks) < chunk_count:
                waiting.insert(0, len(chunks))
        except StopIteration as end:
            momentum_parts[k], blocks = end.value
        for block, flip, _ in blocks:
            place = jnp.bitwise_xor(node, flip)
            weights = lax.dynamic_update_slice(weights, block[None], (place, 0, bounds[k]))
    return weights.reshape(-1, width), jnp.concatenate(momentum_parts, axis=1)


def plan_of(bits, rows):
    if len(bits) < 2 or bits[-1] < 2:
        return [(b, False) for b in bits]
    return [(b, False) for b in bits[:-2]] + [(bits[-2], rows % 16 == 0), (bits[-1], False)]


def local(hidden, cotangent, anchor, momentum, round_mask):
    host_count = lax.axis_size("hst")
    rows = anchor.shape[1]
    branches = []
    for mask in range(1, host_count):
        bits = [b for b in range(host_count.bit_length() - 1) if mask >> b & 1]
        branches.append(lambda *arrays, plan=plan_of(bits, rows): update(plan, *arrays))
    weights, momentum_new = lax.switch(
        round_mask[0] - 1, branches, hidden[0], cotangent[0], anchor[0], momentum[0]
    )
    return (weights[None], momentum_new[None])


def solution(mesh):
    placed = (
        P("hst", "node", None),
        P("hst", "node", None),
        P("hst", "node", None),
        P("hst", "node", None),
        P(),
    )
    return jax.shard_map(
        local,
        mesh=mesh,
        in_specs=placed,
        out_specs=(P("hst", None, None), P("hst", "node", None)),
        check_vma=False,
    )
```

```python
import jax
import jax.numpy as jnp
from jax import lax
from jax.experimental import pallas as pl
from jax.experimental.pallas import tpu as pltpu
from jax.sharding import PartitionSpec as P

base_rate = 0.5
slow_rate = 1.0
slow_beta = 0.7
chunk_shares = (1, 1, 1, 1)


def swapped(block, axis, bit):
    count = lax.axis_size(axis)
    return lax.ppermute(block, axis, [(i, i ^ (1 << bit)) for i in range(count)])


def bit_of(index, bit):
    return jnp.bitwise_and(jnp.right_shift(index, bit), 1)


def wide(block):
    return block.astype(jnp.float32)


def narrow(block):
    return block.astype(jnp.bfloat16)


def partial_products(hidden, cotangent, bounds, scale, turned):
    node_count = lax.axis_size("node")
    tokens = cotangent.shape[0]
    height = hidden.shape[0 if turned else 1]
    rows = height // node_count
    chunk_count = len(bounds) - 1
    widest = 1280 if turned else 512
    tile = max(t for t in range(128, widest + 1, 128) if all(b % t == 0 for b in bounds))
    firsts = [(b - bounds[0]) // tile for b in bounds]

    def kernel(hidden_ref, cotangent_ref, *rest):
        core = jnp.bitwise_and(lax.axis_index("node"), 1)
        step = pl.program_id(0)
        if turned:
            left = hidden_ref
        else:
            left = rest[-1]

            @pl.when(step == 0)
            def _():
                left[...] = hidden_ref[...].T

        product = jnp.dot(left[...], cotangent_ref[...], preferred_element_type=jnp.float32)
        product = narrow(product * scale)
        for chunk in range(chunk_count):

            @pl.when((step >= firsts[chunk]) & (step < firsts[chunk + 1]))
            def _(send_ref=rest[2 * chunk], keep_ref=rest[2 * chunk + 1]):
                for pair in range(node_count // 2):
                    low = product[2 * pair * rows : (2 * pair + 1) * rows]
                    high = product[(2 * pair + 1) * rows : (2 * pair + 2) * rows]
                    send_ref[pair] = jnp.where(core == 1, low, high)
                    keep_ref[pair] = jnp.where(core == 1, high, low)

    shapes, specs = [], []
    for chunk in range(chunk_count):
        first, end = firsts[chunk], firsts[chunk + 1]
        shape = jax.ShapeDtypeStruct((node_count // 2, rows, (end - first) * tile), jnp.bfloat16)
        spec = pl.BlockSpec(
            (node_count // 2, rows, tile),
            lambda j, first=first, end=end: (0, 0, jnp.clip(j, first, end - 1) - first),
        )
        shapes += [shape, shape]
        specs += [spec, spec]
    if not turned:
        shapes.append(jax.ShapeDtypeStruct((height, tokens), jnp.bfloat16))
        specs.append(pl.BlockSpec((height, tokens), lambda j: (0, 0)))
    part = bounds[-1] - bounds[0]
    return pl.pallas_call(
        kernel,
        grid=(part // tile,),
        out_shape=shapes,
        in_specs=[
            pl.BlockSpec(hidden.shape, lambda j: (0, 0)),
            pl.BlockSpec((tokens, tile), lambda j: (0, bounds[0] // tile + j)),
        ],
        out_specs=specs,
        compiler_params=pltpu.CompilerParams(vmem_limit_bytes=32 * 2**20),
        cost_estimate=pl.CostEstimate(
            flops=2 * tokens * height * part,
            bytes_accessed=2 * (tokens * height + tokens * part + height * part),
            transcendentals=0,
        ),
    )(hidden, cotangent)


any_place = pl.BlockSpec(memory_space=pl.ANY)
in_hbm = pl.BlockSpec(memory_space=pltpu.HBM)
in_vmem = pl.BlockSpec(memory_space=pltpu.VMEM)


def small_kernel(body, ins, in_specs, outs, out_specs, scratch=(), aliases=None):
    return pl.pallas_call(
        body,
        out_shape=outs,
        in_specs=in_specs,
        out_specs=out_specs,
        scratch_shapes=list(scratch),
        input_output_aliases=aliases or {},
        compiler_params=pltpu.CompilerParams(vmem_limit_bytes=12 * 2**20),
        cost_estimate=pl.CostEstimate(flops=1024, bytes_accessed=1024, transcendentals=0),
    )(*ins)


def by_rows(count, step):
    @pl.loop(0, count // 16)
    def _(group):
        step(pl.multiple_of(group * 16, 16))


def reduced_over_cores(keep, got, anchor, start):
    rows, part = keep.shape[1:]

    def kernel(keep_ref, got_ref, anchor_ref, send_ref, base_ref, held, sem):
        mine = bit_of(lax.axis_index("node"), 1)
        copy = pltpu.make_async_copy(anchor_ref.at[:, pl.ds(start, part)], held, sem)
        copy.start()

        def for_other(row):
            group = pl.ds(row, 16)
            send_ref[group] = narrow(wide(keep_ref[1 - mine, group]) + wide(got_ref[1 - mine, group]))

        by_rows(rows, for_other)
        copy.wait()

        def for_own(row):
            group = pl.ds(row, 16)
            total = wide(keep_ref[mine, group]) + wide(got_ref[mine, group])
            base_ref[group] = held[group] - base_rate * total

        by_rows(rows, for_own)

    return small_kernel(
        kernel,
        (keep, got, anchor),
        [in_vmem, in_vmem, any_place],
        [jax.ShapeDtypeStruct((rows, part), jnp.bfloat16), jax.ShapeDtypeStruct((rows, part), jnp.float32)],
        [in_vmem, in_vmem],
        [pltpu.VMEM((rows, part), jnp.float32), pltpu.SemaphoreType.DMA],
    )


def met(block, got, factor, gain, in_half, out_half):
    rows, part = got.shape
    sent = rows if out_half is None else rows // 2

    def kernel(block_ref, got_ref, send_ref, sum_ref):
        host = lax.axis_index("hst")
        first = 0 if in_half is None else bit_of(host, in_half) * rows

        def add(row):
            group = pl.ds(row, 16)
            total = block_ref[pl.ds(pl.multiple_of(first + row, 16), 16)] + factor * wide(got_ref[group])
            total = gain * total
            sum_ref[group] = total
            if out_half is None:
                send_ref[group] = narrow(total)

        by_rows(rows, add)
        if out_half is not None:
            other = (1 - bit_of(host, out_half)) * sent

            def give(row):
                send_ref[pl.ds(row, 16)] = narrow(sum_ref[pl.ds(pl.multiple_of(other + row, 16), 16)])

            by_rows(sent, give)

    return small_kernel(
        kernel,
        (block, got),
        [in_vmem, in_vmem],
        [jax.ShapeDtypeStruct((sent, part), jnp.bfloat16), jax.ShapeDtypeStruct((rows, part), jnp.float32)],
        [in_vmem, in_vmem],
    )


def finished(block, got, gain, half, anchor, momentum, momentum_out, start):
    rows = anchor.shape[0]
    part = block.shape[1]
    columns = pl.ds(start, part)

    def kernel(block_ref, got_ref, anchor_ref, momentum_ref, *rest):
        out_ref, fresh_ref, held_anchor, held_momentum, sems = rest[-5:]
        reads = [
            pltpu.make_async_copy(anchor_ref.at[:, columns], held_anchor, sems.at[0]),
            pltpu.make_async_copy(momentum_ref.at[:, columns], held_momentum, sems.at[1]),
        ]
        for read in reads:
            read.start()
        for read in reads:
            read.wait()

        def put(group, averaged):
            old, slow = held_anchor[group], held_momentum[group]
            fresh_ref[group] = narrow(
                (1.0 - slow_rate) * old + slow_rate * averaged - slow_rate * base_rate * slow_beta * slow
            )
            held_momentum[group] = slow_beta * slow + (old - averaged) * (1.0 / base_rate)

        if half is None:
            by_rows(rows, lambda row: put(pl.ds(row, 16), gain * (block_ref[pl.ds(row, 16)] + wide(got_ref[pl.ds(row, 16)]))))
        else:
            count = rows // 2
            mine = bit_of(lax.axis_index("hst"), half) * count
            own, other = mine, count - mine
            by_rows(count, lambda row: put(pl.ds(pl.multiple_of(own + row, 16), 16), block_ref[pl.ds(row, 16)]))
            by_rows(count, lambda row: put(pl.ds(pl.multiple_of(other + row, 16), 16), wide(got_ref[pl.ds(row, 16)])))
        write = pltpu.make_async_copy(held_momentum, out_ref.at[:, columns], sems.at[0])
        write.start()
        write.wait()

    held = [] if momentum_out is None else [momentum_out]
    momentum_out, fresh = small_kernel(
        kernel,
        (block, got, anchor, momentum, *held),
        [in_vmem, in_vmem, any_place, any_place] + [in_hbm] * len(held),
        [jax.ShapeDtypeStruct(anchor.shape, jnp.float32), jax.ShapeDtypeStruct((rows, part), jnp.bfloat16)],
        [in_hbm, in_vmem],
        [pltpu.VMEM((rows, part), jnp.float32)] * 2 + [pltpu.SemaphoreType.DMA((2,))],
        {4: 0} if held else None,
    )
    return fresh, momentum_out


def placed_in(weights, shape, blocks, flips, start):
    part = blocks[0].shape[1]

    def kernel(*refs):
        out_ref, sems = refs[-2:]
        node = lax.axis_index("node")
        copies = [
            pltpu.make_async_copy(
                refs[i], out_ref.at[jnp.bitwise_xor(node, flip), :, pl.ds(start, part)], sems.at[i]
            )
            for i, flip in enumerate(flips)
        ]
        for copy in copies:
            copy.start()
        for copy in copies:
            copy.wait()

    held = [] if weights is None else [weights]
    return small_kernel(
        kernel,
        (*blocks, *held),
        [in_vmem] * len(blocks) + [in_hbm] * len(held),
        [jax.ShapeDtypeStruct(shape, jnp.bfloat16)],
        [in_hbm],
        [pltpu.SemaphoreType.DMA((len(blocks),))],
        {len(blocks): 0} if held else None,
    )[0]


def chunk_steps(plan, k, gates, base, got, start, shared):
    if got is None:
        (got,) = yield [(gates[k], "node", 1)]
    block, factor, in_half = base, -base_rate, None
    halved = []
    gain = 1.0 / (1 << len(plan))
    for place, (bit, by_halves) in enumerate(plan):
        send, block = met(block, got, factor, 1.0, in_half, bit if by_halves else None)
        (got,) = yield [(send, "hst", bit)]
        factor, in_half = 1.0, bit if by_halves else None
        halved += [bit] * by_halves
    half = None
    if halved:
        (half,) = halved
        send, block = met(block, got, factor, gain, in_half, None)
        (got,) = yield [(send, "hst", half)]
    fresh, shared["momentum"] = finished(
        block, got, gain, half, shared["anchor"], shared["momentum_in"], shared["momentum"], start
    )
    over_y, over_core = yield [(fresh, "node", 1), (fresh, "node", 0)]
    shape = shared["shape"]
    shared["weights"] = placed_in(shared["weights"], shape, [fresh, over_core, over_y], [0, 1, 2], start)
    (over_both,) = yield [(over_y, "node", 0)]
    shared["weights"] = placed_in(shared["weights"], shape, [over_both], [3], start)


def update(plan, bounds, anchor, momentum, arrived_first, *sends_and_bases):
    rows, width = anchor.shape
    node_count = lax.axis_size("node")
    shared = {
        "anchor": anchor, "momentum_in": momentum, "momentum": None, "weights": None, "shape": (node_count, rows, width),
    }
    bases, sends = list(sends_and_bases[0::2]), list(sends_and_bases[1::2])
    arrived_first, sends = lax.optimization_barrier((arrived_first, sends))
    got = [arrived_first] + [None] * (len(bases) - 1)
    gates = [None] + sends
    chunks = [
        chunk_steps(plan, k, gates, base, g, start, shared)
        for k, (base, g, start) in enumerate(zip(bases, got, bounds))
    ]
    arrived = [None] * len(chunks)
    last = None
    begun = set()
    waiting = list(range(1, len(chunks)))
    waiting = waiting[:1] + [0] + waiting[1:]
    while waiting:
        k = waiting.pop(0)
        if k in begun:
            held = {name: shared[name] for name in ("weights", "momentum") if shared[name] is not None}
            arrived[k], last, held = lax.optimization_barrier((arrived[k], last, held))
            shared.update(held)
        elif k > 1:
            gates[k], last = lax.optimization_barrier((gates[k], last))
        begun.add(k)
        try:
            moves = chunks[k].send(arrived[k])
            last = [a for a, *_ in moves]
            arrived[k] = [swapped(*move) for move in moves]
            waiting.append(k)
        except StopIteration:
            pass
    return shared["weights"].reshape(-1, width), shared["momentum"]


def plan_of(bits):
    if len(bits) < 2 or bits[-1] < 2:
        return [(b, False) for b in bits]
    return [(b, False) for b in bits[:-2]] + [(bits[-2], True), (bits[-1], False)]


def local(hidden, cotangent, anchor, momentum, round_mask):
    hidden, cotangent, anchor, momentum = hidden[0], cotangent[0], anchor[0], momentum[0]
    tokens, width = cotangent.shape
    node_count, host_count = lax.axis_size("node"), lax.axis_size("hst")
    scale = 1.0 / (tokens * node_count)
    unit = width // sum(chunk_shares)
    bounds = [unit * sum(chunk_shares[:k]) for k in range(len(chunk_shares) + 1)]
    send, keep, left = partial_products(hidden, cotangent, bounds[:2], scale, turned=False)
    send, base = reduced_over_cores(keep, swapped(send, "node", 0), anchor, 0)
    send, left = lax.optimization_barrier((send, left))
    arrived_first = swapped(send, "node", 1)
    parts = partial_products(left, cotangent, bounds[1:], scale, turned=True)
    handed = [base]
    for k in range(1, len(chunk_shares)):
        handed += reduced_over_cores(parts[2 * k - 1], swapped(parts[2 * k - 2], "node", 0), anchor, bounds[k])
    branches = []
    for mask in range(1, host_count):
        bits = [b for b in range(host_count.bit_length() - 1) if mask >> b & 1]
        branches.append(lambda *arrays, plan=plan_of(bits): update(plan, bounds, *arrays))
    weights, momentum_new = lax.switch(
        round_mask[0] - 1, branches, anchor, momentum, arrived_first, *handed
    )
    return (weights[None], momentum_new[None])


def solution(mesh):
    placed = (
        P("hst", "node", None),
        P("hst", "node", None),
        P("hst", "node", None),
        P("hst", "node", None),
        P(),
    )
    return jax.shard_map(
        local,
        mesh=mesh,
        in_specs=placed,
        out_specs=(P("hst", None, None), P("hst", "node", None)),
        check_vma=False,
    )
```

```python
import jax
import jax.numpy as jnp
from jax import lax
from jax.experimental import pallas as pl
from jax.experimental.pallas import tpu as pltpu
from jax.sharding import PartitionSpec as P

base_rate = 0.5
slow_rate = 1.0
slow_beta = 0.7
chunk_count = 4


def swapped(block, axis, bit):
    count = lax.axis_size(axis)
    return lax.ppermute(block, axis, [(i, i ^ (1 << bit)) for i in range(count)])


def bit_of(index, bit):
    return jnp.bitwise_and(jnp.right_shift(index, bit), 1)


def wide(block):
    return block.astype(jnp.float32)


def narrow(block):
    return block.astype(jnp.bfloat16)


any_place = pl.BlockSpec(memory_space=pl.ANY)
in_hbm = pl.BlockSpec(memory_space=pltpu.HBM)
in_vmem = pl.BlockSpec(memory_space=pltpu.VMEM)


def partial_products(hidden, cotangent, bounds, tile, scale, turned):
    node_count = lax.axis_size("node")
    tokens = cotangent.shape[0]
    height = hidden.shape[0 if turned else 1]
    rows = height // node_count
    chunk_count = len(bounds) - 1
    tiles = (bounds[1] - bounds[0]) // tile
    count = tiles * chunk_count

    def kernel(hidden_ref, cotangent_ref, *rest):
        core = jnp.bitwise_and(lax.axis_index("node"), 1)
        fetched, sems = rest[-2:]

        def fetch(step):
            columns = pl.ds(pl.multiple_of(bounds[0] + step * tile, 128), tile)
            return pltpu.make_async_copy(cotangent_ref.at[:, columns], fetched.at[step], sems.at[step])

        if turned:
            left = hidden_ref
            for step in range(count):
                fetch(step).start()
        else:
            left, straight, straight_sem = rest[2 * chunk_count : 2 * chunk_count + 3]
            copy = pltpu.make_async_copy(hidden_ref, straight, straight_sem)
            copy.start()
            for step in range(count):
                fetch(step).start()
            copy.wait()
            left[...] = straight[...].T

        @pl.loop(0, count)
        def _(step):
            fetch(step).wait()
            product = jnp.dot(left[...], fetched[step], preferred_element_type=jnp.float32)
            product = narrow(product * scale)
            for chunk in range(chunk_count):

                @pl.when((step >= chunk * tiles) & (step < (chunk + 1) * tiles))
                def _(send_ref=rest[2 * chunk], keep_ref=rest[2 * chunk + 1]):
                    columns = pl.ds(pl.multiple_of((step - chunk * tiles) * tile, 128), tile)
                    for pair in range(node_count // 2):
                        low = product[2 * pair * rows : (2 * pair + 1) * rows]
                        high = product[(2 * pair + 1) * rows : (2 * pair + 2) * rows]
                        send_ref[pair, :, columns] = jnp.where(core == 1, low, high)
                        keep_ref[pair, :, columns] = jnp.where(core == 1, high, low)

    part = bounds[-1] - bounds[0]
    half = jax.ShapeDtypeStruct((node_count // 2, rows, part // chunk_count), jnp.bfloat16)
    shapes = [half] * (2 * chunk_count)
    scratch = []
    if not turned:
        shapes.append(jax.ShapeDtypeStruct((height, tokens), jnp.bfloat16))
        scratch = [pltpu.VMEM(hidden.shape, jnp.bfloat16), pltpu.SemaphoreType.DMA]
    return pl.pallas_call(
        kernel,
        out_shape=shapes,
        in_specs=[in_vmem if turned else in_hbm, in_hbm],
        out_specs=[in_vmem] * len(shapes),
        scratch_shapes=scratch + [pltpu.VMEM((count, tokens, tile), jnp.bfloat16), pltpu.SemaphoreType.DMA((count,))],
        compiler_params=pltpu.CompilerParams(vmem_limit_bytes=56 * 2**20),
        cost_estimate=pl.CostEstimate(
            flops=2 * tokens * height * part,
            bytes_accessed=2 * (tokens * height + tokens * part + height * part),
            transcendentals=0,
        ),
    )(hidden, cotangent)


def small_kernel(body, ins, in_specs, outs, out_specs, scratch=(), aliases=None):
    return pl.pallas_call(
        body,
        out_shape=outs,
        in_specs=in_specs,
        out_specs=out_specs,
        scratch_shapes=list(scratch),
        input_output_aliases=aliases or {},
        compiler_params=pltpu.CompilerParams(vmem_limit_bytes=12 * 2**20),
        cost_estimate=pl.CostEstimate(flops=1024, bytes_accessed=1024, transcendentals=0),
    )(*ins)


def by_rows(count, step):
    @pl.loop(0, count // 16)
    def _(group):
        step(pl.multiple_of(group * 16, 16))


def reduced_over_cores(keep, got, anchor, start):
    rows, part = keep.shape[1:]

    def kernel(keep_ref, got_ref, anchor_ref, send_ref, base_ref, held, sem):
        mine = bit_of(lax.axis_index("node"), 1)
        copy = pltpu.make_async_copy(anchor_ref.at[:, pl.ds(start, part)], held, sem)
        copy.start()

        def for_other(row):
            group = pl.ds(row, 16)
            send_ref[group] = narrow(wide(keep_ref[1 - mine, group]) + wide(got_ref[1 - mine, group]))

        by_rows(rows, for_other)
        copy.wait()

        def for_own(row):
            group = pl.ds(row, 16)
            total = wide(keep_ref[mine, group]) + wide(got_ref[mine, group])
            base_ref[group] = held[group] - base_rate * total

        by_rows(rows, for_own)

    return small_kernel(
        kernel,
        (keep, got, anchor),
        [in_vmem, in_vmem, any_place],
        [jax.ShapeDtypeStruct((rows, part), jnp.bfloat16), jax.ShapeDtypeStruct((rows, part), jnp.float32)],
        [in_vmem, in_vmem],
        [pltpu.VMEM((rows, part), jnp.float32), pltpu.SemaphoreType.DMA],
    )


def met(block, got, factor, gain, in_half, out_half):
    rows, part = got.shape
    sent = rows if out_half is None else rows // 2

    def kernel(block_ref, got_ref, send_ref, sum_ref):
        host = lax.axis_index("hst")
        first = 0 if in_half is None else bit_of(host, in_half) * rows

        def add(row):
            group = pl.ds(row, 16)
            total = block_ref[pl.ds(pl.multiple_of(first + row, 16), 16)] + factor * wide(got_ref[group])
            total = gain * total
            sum_ref[group] = total
            if out_half is None:
                send_ref[group] = narrow(total)

        by_rows(rows, add)
        if out_half is not None:
            other = (1 - bit_of(host, out_half)) * sent

            def give(row):
                send_ref[pl.ds(row, 16)] = narrow(sum_ref[pl.ds(pl.multiple_of(other + row, 16), 16)])

            by_rows(sent, give)

    return small_kernel(
        kernel,
        (block, got),
        [in_vmem, in_vmem],
        [jax.ShapeDtypeStruct((sent, part), jnp.bfloat16), jax.ShapeDtypeStruct((rows, part), jnp.float32)],
        [in_vmem, in_vmem],
    )


def finished(block, got, gain, half, anchor, momentum, momentum_out, start):
    rows = anchor.shape[0]
    part = block.shape[1]
    columns = pl.ds(start, part)

    def kernel(block_ref, got_ref, anchor_ref, momentum_ref, *rest):
        out_ref, fresh_ref, held_anchor, held_momentum, sems = rest[-5:]
        reads = [
            pltpu.make_async_copy(anchor_ref.at[:, columns], held_anchor, sems.at[0]),
            pltpu.make_async_copy(momentum_ref.at[:, columns], held_momentum, sems.at[1]),
        ]
        for read in reads:
            read.start()
        for read in reads:
            read.wait()

        def put(group, averaged):
            old, slow = held_anchor[group], held_momentum[group]
            fresh_ref[group] = narrow(
                (1.0 - slow_rate) * old + slow_rate * averaged - slow_rate * base_rate * slow_beta * slow
            )
            held_momentum[group] = slow_beta * slow + (old - averaged) * (1.0 / base_rate)

        if half is None:
            by_rows(rows, lambda row: put(pl.ds(row, 16), gain * (block_ref[pl.ds(row, 16)] + wide(got_ref[pl.ds(row, 16)]))))
        else:
            count = rows // 2
            mine = bit_of(lax.axis_index("hst"), half) * count
            own, other = mine, count - mine
            by_rows(count, lambda row: put(pl.ds(pl.multiple_of(own + row, 16), 16), block_ref[pl.ds(row, 16)]))
            by_rows(count, lambda row: put(pl.ds(pl.multiple_of(other + row, 16), 16), wide(got_ref[pl.ds(row, 16)])))
        write = pltpu.make_async_copy(held_momentum, out_ref.at[:, columns], sems.at[0])
        write.start()
        write.wait()

    held = [] if momentum_out is None else [momentum_out]
    momentum_out, fresh = small_kernel(
        kernel,
        (block, got, anchor, momentum, *held),
        [in_vmem, in_vmem, any_place, any_place] + [in_hbm] * len(held),
        [jax.ShapeDtypeStruct(anchor.shape, jnp.float32), jax.ShapeDtypeStruct((rows, part), jnp.bfloat16)],
        [in_hbm, in_vmem],
        [pltpu.VMEM((rows, part), jnp.float32)] * 2 + [pltpu.SemaphoreType.DMA((2,))],
        {4: 0} if held else None,
    )
    return fresh, momentum_out


def placed_in(weights, shape, pieces):
    blocks = [block for block, _, _ in pieces]

    def kernel(*refs):
        out_ref, sems = refs[-2:]
        node = lax.axis_index("node")
        copies = [
            pltpu.make_async_copy(
                refs[i], out_ref.at[jnp.bitwise_xor(node, flip), :, pl.ds(start, block.shape[1])], sems.at[i]
            )
            for i, (block, flip, start) in enumerate(pieces)
        ]
        for copy in copies:
            copy.start()
        for copy in copies:
            copy.wait()

    held = [] if weights is None else [weights]
    return small_kernel(
        kernel,
        (*blocks, *held),
        [in_vmem] * len(blocks) + [in_hbm] * len(held),
        [jax.ShapeDtypeStruct(shape, jnp.bfloat16)],
        [in_hbm],
        [pltpu.SemaphoreType.DMA((len(blocks),))],
        {len(blocks): 0} if held else None,
    )[0]


def chunk_steps(plan, send, base, start, shared):
    (got,) = yield [(send, "node", 1)]
    block, factor, in_half = base, -base_rate, None
    halved = []
    gain = 1.0 / (1 << len(plan))
    for place, (bit, by_halves) in enumerate(plan):
        send, block = met(block, got, factor, 1.0, in_half, bit if by_halves else None)
        (got,) = yield [(send, "hst", bit)]
        factor, in_half = 1.0, bit if by_halves else None
        halved += [bit] * by_halves
    half = None
    if halved:
        (half,) = halved
        send, block = met(block, got, factor, gain, in_half, None)
        (got,) = yield [(send, "hst", half)]
    fresh, shared["momentum"] = finished(
        block, got, gain, half, shared["anchor"], shared["momentum_in"], shared["momentum"], start
    )
    over_y, over_core = yield [(fresh, "node", 1), (fresh, "node", 0)]
    pieces = [(fresh, 0, start), (over_core, 1, start), (over_y, 2, start), *shared["late"]]
    shared["late"] = [(swapped(over_y, "node", 0), 3, start)]
    shared["weights"] = placed_in(shared["weights"], shared["shape"], pieces)


def update(plan, bounds, anchor, momentum, *sends_and_bases):
    rows, width = anchor.shape
    node_count = lax.axis_size("node")
    shared = {
        "anchor": anchor, "momentum_in": momentum, "momentum": None, "weights": None, "late": [],
        "shape": (node_count, rows, width),
    }
    sends, bases = sends_and_bases[0::2], sends_and_bases[1::2]
    chunks = [
        chunk_steps(plan, send, base, start, shared) for send, base, start in zip(sends, bases, bounds)
    ]
    arrived = [None] * len(chunks)
    last = None
    waiting = list(range(len(chunks)))
    while waiting:
        k = waiting.pop(0)
        if arrived[k] is not None:
            held = {name: shared[name] for name in ("weights", "momentum") if shared[name] is not None}
            arrived[k], last, held = lax.optimization_barrier((arrived[k], last, held))
            shared.update(held)
        try:
            moves = chunks[k].send(arrived[k])
            last = [a for a, *_ in moves]
            arrived[k] = [swapped(*move) for move in moves]
            waiting.append(k)
        except StopIteration:
            pass
    weights = placed_in(shared["weights"], shared["shape"], shared["late"])
    return weights.reshape(-1, width), shared["momentum"]


def plan_of(bits):
    if len(bits) < 2 or bits[-1] < 2:
        return [(b, False) for b in bits]
    return [(b, False) for b in bits[:-2]] + [(bits[-2], True), (bits[-1], False)]


def local(hidden, cotangent, anchor, momentum, round_mask):
    hidden, cotangent, anchor, momentum = hidden[0], cotangent[0], anchor[0], momentum[0]
    tokens, width = cotangent.shape
    node_count, host_count = lax.axis_size("node"), lax.axis_size("hst")
    scale = 1.0 / (tokens * node_count)
    unit = width // chunk_count
    bounds = [unit * k for k in range(chunk_count + 1)]
    middle = chunk_count // 2
    *first, left = partial_products(hidden, cotangent, bounds[: middle + 1], unit, scale, turned=False)
    first_gots = [swapped(part, "node", 0) for part in first[0::2]]
    later = partial_products(left, cotangent, bounds[middle:], unit, scale, turned=True)
    first_gots, later_sends = lax.optimization_barrier((first_gots, later[0::2]))
    gots = [*first_gots, *(swapped(part, "node", 0) for part in later_sends)]
    handed = []
    for keep, got, start in zip([*first[1::2], *later[1::2]], gots, bounds):
        handed += reduced_over_cores(keep, got, anchor, start)
    branches = []
    for mask in range(1, host_count):
        bits = [b for b in range(host_count.bit_length() - 1) if mask >> b & 1]
        branches.append(lambda *arrays, plan=plan_of(bits): update(plan, bounds, *arrays))
    weights, momentum_new = lax.switch(
        round_mask[0] - 1, branches, anchor, momentum, *handed
    )
    return (weights[None], momentum_new[None])


def solution(mesh):
    placed = (
        P("hst", "node", None),
        P("hst", "node", None),
        P("hst", "node", None),
        P("hst", "node", None),
        P(),
    )
    return jax.shard_map(
        local,
        mesh=mesh,
        in_specs=placed,
        out_specs=(P("hst", None, None), P("hst", "node", None)),
        check_vma=False,
    )
```

```python
import jax
import jax.numpy as jnp
from jax import lax
from jax.experimental import pallas as pl
from jax.experimental.pallas import tpu as pltpu
from jax.sharding import PartitionSpec as P

base_rate = 0.5
slow_rate = 1.0
slow_beta = 0.7
chunk_count = 4


def swapped(block, axis, bit):
    count = lax.axis_size(axis)
    return lax.ppermute(block, axis, [(i, i ^ (1 << bit)) for i in range(count)])


def bit_of(index, bit):
    return jnp.bitwise_and(jnp.right_shift(index, bit), 1)


def wide(block):
    return block.astype(jnp.float32)


def narrow(block):
    return block.astype(jnp.bfloat16)


any_place = pl.BlockSpec(memory_space=pl.ANY)
in_hbm = pl.BlockSpec(memory_space=pltpu.HBM)
in_vmem = pl.BlockSpec(memory_space=pltpu.VMEM)


def partial_products(hidden, cotangent, bounds, scale, turned):
    node_count = lax.axis_size("node")
    tokens = cotangent.shape[0]
    height = hidden.shape[0 if turned else 1]
    rows = height // node_count
    count = len(bounds) - 1
    tile = bounds[1] - bounds[0]

    def kernel(hidden_ref, cotangent_ref, *rest):
        core = jnp.bitwise_and(lax.axis_index("node"), 1)
        fetched, sems = rest[-2:]

        def fetch(step):
            columns = pl.ds(bounds[step], tile)
            return pltpu.make_async_copy(cotangent_ref.at[:, columns], fetched.at[step], sems.at[step])

        if turned:
            left = hidden_ref
            for step in range(count):
                fetch(step).start()
        else:
            left, straight, straight_sem = rest[2 * count : 2 * count + 3]
            copy = pltpu.make_async_copy(hidden_ref, straight, straight_sem)
            copy.start()
            for step in range(count):
                fetch(step).start()
            copy.wait()
            left[...] = straight[...].T

        for step in range(count):
            fetch(step).wait()
            product = jnp.dot(left[...], fetched[step], preferred_element_type=jnp.float32)
            product = narrow(product * scale)
            send_ref, keep_ref = rest[2 * step : 2 * step + 2]
            for pair in range(node_count // 2):
                low = product[2 * pair * rows : (2 * pair + 1) * rows]
                high = product[(2 * pair + 1) * rows : (2 * pair + 2) * rows]
                send_ref[pair] = jnp.where(core == 1, low, high)
                keep_ref[pair] = jnp.where(core == 1, high, low)

    part = bounds[-1] - bounds[0]
    half = jax.ShapeDtypeStruct((node_count // 2, rows, tile), jnp.bfloat16)
    shapes = [half] * (2 * count)
    scratch = []
    if not turned:
        shapes.append(jax.ShapeDtypeStruct((height, tokens), jnp.bfloat16))
        scratch = [pltpu.VMEM(hidden.shape, jnp.bfloat16), pltpu.SemaphoreType.DMA]
    return pl.pallas_call(
        kernel,
        out_shape=shapes,
        in_specs=[in_vmem if turned else in_hbm, in_hbm],
        out_specs=[in_vmem] * len(shapes),
        scratch_shapes=scratch + [pltpu.VMEM((count, tokens, tile), jnp.bfloat16), pltpu.SemaphoreType.DMA((count,))],
        compiler_params=pltpu.CompilerParams(vmem_limit_bytes=56 * 2**20),
        cost_estimate=pl.CostEstimate(
            flops=2 * tokens * height * part,
            bytes_accessed=2 * (tokens * height + tokens * part + height * part),
            transcendentals=0,
        ),
    )(hidden, cotangent)


def small_kernel(body, ins, in_specs, outs, out_specs, scratch=(), aliases=None):
    return pl.pallas_call(
        body,
        out_shape=outs,
        in_specs=in_specs,
        out_specs=out_specs,
        scratch_shapes=list(scratch),
        input_output_aliases=aliases or {},
        compiler_params=pltpu.CompilerParams(vmem_limit_bytes=12 * 2**20),
        cost_estimate=pl.CostEstimate(flops=1024, bytes_accessed=1024, transcendentals=0),
    )(*ins)


def by_rows(count, step):
    @pl.loop(0, count // 16)
    def _(group):
        step(pl.multiple_of(group * 16, 16))


def reduced_over_cores(keep, got, anchor, start):
    rows, part = keep.shape[1:]

    def kernel(keep_ref, got_ref, anchor_ref, send_ref, base_ref, held, sem):
        mine = bit_of(lax.axis_index("node"), 1)
        copy = pltpu.make_async_copy(anchor_ref.at[:, pl.ds(start, part)], held, sem)
        copy.start()

        def for_other(row):
            group = pl.ds(row, 16)
            send_ref[group] = narrow(wide(keep_ref[1 - mine, group]) + wide(got_ref[1 - mine, group]))

        by_rows(rows, for_other)
        copy.wait()

        def for_own(row):
            group = pl.ds(row, 16)
            total = wide(keep_ref[mine, group]) + wide(got_ref[mine, group])
            base_ref[group] = held[group] - base_rate * total

        by_rows(rows, for_own)

    return small_kernel(
        kernel,
        (keep, got, anchor),
        [in_vmem, in_vmem, any_place],
        [jax.ShapeDtypeStruct((rows, part), jnp.bfloat16), jax.ShapeDtypeStruct((rows, part), jnp.float32)],
        [in_vmem, in_vmem],
        [pltpu.VMEM((rows, part), jnp.float32), pltpu.SemaphoreType.DMA],
    )


def met(block, got, factor, gain, in_half, out_half):
    rows, part = got.shape
    sent = rows if out_half is None else rows // 2

    def kernel(block_ref, got_ref, send_ref, sum_ref):
        host = lax.axis_index("hst")
        first = 0 if in_half is None else bit_of(host, in_half) * rows

        def add(row):
            group = pl.ds(row, 16)
            total = block_ref[pl.ds(pl.multiple_of(first + row, 16), 16)] + factor * wide(got_ref[group])
            total = gain * total
            sum_ref[group] = total
            if out_half is None:
                send_ref[group] = narrow(total)

        by_rows(rows, add)
        if out_half is not None:
            other = (1 - bit_of(host, out_half)) * sent

            def give(row):
                send_ref[pl.ds(row, 16)] = narrow(sum_ref[pl.ds(pl.multiple_of(other + row, 16), 16)])

            by_rows(sent, give)

    return small_kernel(
        kernel,
        (block, got),
        [in_vmem, in_vmem],
        [jax.ShapeDtypeStruct((sent, part), jnp.bfloat16), jax.ShapeDtypeStruct((rows, part), jnp.float32)],
        [in_vmem, in_vmem],
    )


def finished(block, got, gain, half, anchor, momentum, momentum_out, start):
    rows = anchor.shape[0]
    part = block.shape[1]
    columns = pl.ds(start, part)

    def kernel(block_ref, got_ref, anchor_ref, momentum_ref, *rest):
        out_ref, fresh_ref, held_anchor, held_momentum, sems = rest[-5:]
        reads = [
            pltpu.make_async_copy(anchor_ref.at[:, columns], held_anchor, sems.at[0]),
            pltpu.make_async_copy(momentum_ref.at[:, columns], held_momentum, sems.at[1]),
        ]
        for read in reads:
            read.start()
        for read in reads:
            read.wait()

        def put(group, averaged):
            old, slow = held_anchor[group], held_momentum[group]
            fresh_ref[group] = narrow(
                (1.0 - slow_rate) * old + slow_rate * averaged - slow_rate * base_rate * slow_beta * slow
            )
            held_momentum[group] = slow_beta * slow + (old - averaged) * (1.0 / base_rate)

        if half is None:
            by_rows(rows, lambda row: put(pl.ds(row, 16), gain * (block_ref[pl.ds(row, 16)] + wide(got_ref[pl.ds(row, 16)]))))
        else:
            count = rows // 2
            mine = bit_of(lax.axis_index("hst"), half) * count
            own, other = mine, count - mine
            by_rows(count, lambda row: put(pl.ds(pl.multiple_of(own + row, 16), 16), block_ref[pl.ds(row, 16)]))
            by_rows(count, lambda row: put(pl.ds(pl.multiple_of(other + row, 16), 16), wide(got_ref[pl.ds(row, 16)])))
        write = pltpu.make_async_copy(held_momentum, out_ref.at[:, columns], sems.at[0])
        write.start()
        write.wait()

    held = [] if momentum_out is None else [momentum_out]
    momentum_out, fresh = small_kernel(
        kernel,
        (block, got, anchor, momentum, *held),
        [in_vmem, in_vmem, any_place, any_place] + [in_hbm] * len(held),
        [jax.ShapeDtypeStruct(anchor.shape, jnp.float32), jax.ShapeDtypeStruct((rows, part), jnp.bfloat16)],
        [in_hbm, in_vmem],
        [pltpu.VMEM((rows, part), jnp.float32)] * 2 + [pltpu.SemaphoreType.DMA((2,))],
        {4: 0} if held else None,
    )
    return fresh, momentum_out


def placed_in(weights, shape, pieces):
    blocks = [block for block, _, _ in pieces]

    def kernel(*refs):
        out_ref, sems = refs[-2:]
        node = lax.axis_index("node")
        copies = [
            pltpu.make_async_copy(
                refs[i], out_ref.at[jnp.bitwise_xor(node, flip), :, pl.ds(start, block.shape[1])], sems.at[i]
            )
            for i, (block, flip, start) in enumerate(pieces)
        ]
        for copy in copies:
            copy.start()
        for copy in copies:
            copy.wait()

    held = [] if weights is None else [weights]
    return small_kernel(
        kernel,
        (*blocks, *held),
        [in_vmem] * len(blocks) + [in_hbm] * len(held),
        [jax.ShapeDtypeStruct(shape, jnp.bfloat16)],
        [in_hbm],
        [pltpu.SemaphoreType.DMA((len(blocks),))],
        {len(blocks): 0} if held else None,
    )[0]


def chunk_steps(plan, sends, k, base, start, shared):
    (got,) = yield [(sends[k], "node", 1)]
    block, factor, in_half = base, -base_rate, None
    halved = []
    gain = 1.0 / (1 << len(plan))
    for place, (bit, by_halves) in enumerate(plan):
        send, block = met(block, got, factor, 1.0, in_half, bit if by_halves else None)
        (got,) = yield [(send, "hst", bit)]
        factor, in_half = 1.0, bit if by_halves else None
        halved += [bit] * by_halves
    half = None
    if halved:
        (half,) = halved
        send, block = met(block, got, factor, gain, in_half, None)
        (got,) = yield [(send, "hst", half)]
    fresh, shared["momentum"] = finished(
        block, got, gain, half, shared["anchor"], shared["momentum_in"], shared["momentum"], start
    )
    over_y, over_core = yield [(fresh, "node", 1), (fresh, "node", 0)]
    pieces = [(fresh, 0, start), (over_core, 1, start), (over_y, 2, start), *shared["late"]]
    shared["late"] = [(swapped(over_y, "node", 0), 3, start)]
    shared["weights"] = placed_in(shared["weights"], shared["shape"], pieces)


def update(plan, bounds, anchor, momentum, *sends_and_bases):
    rows, width = anchor.shape
    node_count = lax.axis_size("node")
    shared = {
        "anchor": anchor, "momentum_in": momentum, "momentum": None, "weights": None, "late": [],
        "shape": (node_count, rows, width),
    }
    sends, bases = list(sends_and_bases[0::2]), sends_and_bases[1::2]
    chunks = [chunk_steps(plan, sends, k, bases[k], bounds[k], shared) for k in range(len(bases))]
    arrived = [None] * len(chunks)
    last = None
    waiting = list(range(len(chunks)))
    waiting, later = waiting[:2], waiting[2:]
    steps = [0] * len(chunks)
    while waiting:
        k = waiting.pop(0)
        if arrived[k] is not None:
            held = {name: shared[name] for name in ("weights", "momentum") if shared[name] is not None}
            arrived[k], last, held = lax.optimization_barrier((arrived[k], last, held))
            shared.update(held)
        elif last is not None:
            sends[k], last = lax.optimization_barrier((sends[k], last))
        try:
            moves = chunks[k].send(arrived[k])
            last = [a for a, *_ in moves]
            arrived[k] = [swapped(*move) for move in moves]
            waiting.append(k)
            if steps[k] == 1 and later:
                waiting.insert(0, later.pop(0))
            steps[k] += 1
        except StopIteration:
            pass
    weights = placed_in(shared["weights"], shared["shape"], shared["late"])
    return weights.reshape(-1, width), shared["momentum"]


def plan_of(bits):
    if len(bits) < 2 or bits[-1] < 2:
        return [(b, False) for b in bits]
    return [(b, False) for b in bits[:-2]] + [(bits[-2], True), (bits[-1], False)]


def local(hidden, cotangent, anchor, momentum, round_mask):
    hidden, cotangent, anchor, momentum = hidden[0], cotangent[0], anchor[0], momentum[0]
    tokens, width = cotangent.shape
    node_count, host_count = lax.axis_size("node"), lax.axis_size("hst")
    scale = 1.0 / (tokens * node_count)
    unit = width // chunk_count
    bounds = [unit * k for k in range(chunk_count + 1)]
    middle = chunk_count // 2
    *first, left = partial_products(hidden, cotangent, bounds[: middle + 1], scale, turned=False)
    first_gots = [swapped(part, "node", 0) for part in first[0::2]]
    later = partial_products(left, cotangent, bounds[middle:], scale, turned=True)
    first_gots, later_sends = lax.optimization_barrier((first_gots, later[0::2]))
    gots = [*first_gots, *(swapped(part, "node", 0) for part in later_sends)]
    handed = []
    for keep, got, start in zip([*first[1::2], *later[1::2]], gots, bounds):
        handed += reduced_over_cores(keep, got, anchor, start)
    branches = []
    for mask in range(1, host_count):
        bits = [b for b in range(host_count.bit_length() - 1) if mask >> b & 1]
        branches.append(lambda *arrays, plan=plan_of(bits): update(plan, bounds, *arrays))
    weights, momentum_new = lax.switch(
        round_mask[0] - 1, branches, anchor, momentum, *handed
    )
    return (weights[None], momentum_new[None])


def solution(mesh):
    placed = (
        P("hst", "node", None),
        P("hst", "node", None),
        P("hst", "node", None),
        P("hst", "node", None),
        P(),
    )
    return jax.shard_map(
        local,
        mesh=mesh,
        in_specs=placed,
        out_specs=(P("hst", None, None), P("hst", "node", None)),
        check_vma=False,
    )
```

```python
import jax
import jax.numpy as jnp
from jax import lax
from jax.experimental import pallas as pl
from jax.experimental.pallas import tpu as pltpu
from jax.sharding import PartitionSpec as P

base_rate = 0.5
slow_rate = 1.0
slow_beta = 0.7
chunk_count = 4


def swapped(block, axis, bit):
    count = lax.axis_size(axis)
    return lax.ppermute(block, axis, [(i, i ^ (1 << bit)) for i in range(count)])


def bit_of(index, bit):
    return jnp.bitwise_and(jnp.right_shift(index, bit), 1)


def wide(block):
    return block.astype(jnp.float32)


def narrow(block):
    return block.astype(jnp.bfloat16)


any_place = pl.BlockSpec(memory_space=pl.ANY)
in_hbm = pl.BlockSpec(memory_space=pltpu.HBM)
in_vmem = pl.BlockSpec(memory_space=pltpu.VMEM)


def small_kernel(body, ins, in_specs, outs, out_specs, scratch=(), aliases=None):
    return pl.pallas_call(
        body,
        out_shape=outs,
        in_specs=in_specs,
        out_specs=out_specs,
        scratch_shapes=list(scratch),
        input_output_aliases=aliases or {},
        compiler_params=pltpu.CompilerParams(vmem_limit_bytes=12 * 2**20),
        cost_estimate=pl.CostEstimate(flops=1024, bytes_accessed=1024, transcendentals=0),
    )(*ins)


def by_rows(count, step):
    @pl.loop(0, count // 16)
    def _(group):
        step(pl.multiple_of(group * 16, 16))


def split_by_core(product, node_count, count):
    rows, part = product.shape[0] // node_count, product.shape[1] // count

    def kernel(product_ref, *outs):
        core = bit_of(lax.axis_index("node"), 0)
        for chunk in range(count):
            for pair in range(node_count // 2):
                for out_ref, first in zip(outs[2 * chunk : 2 * chunk + 2], (1 - core, core)):

                    def move(row, out_ref=out_ref, first=first, chunk=chunk, pair=pair):
                        source = pl.ds(pl.multiple_of((2 * pair + first) * rows + row, 16), 16)
                        out_ref[pair, pl.ds(row, 16)] = product_ref[source, chunk * part : (chunk + 1) * part]

                    by_rows(rows, move)

    half = jax.ShapeDtypeStruct((node_count // 2, rows, part), jnp.bfloat16)
    return small_kernel(kernel, (product,), [in_vmem], [half] * (2 * count), [in_vmem] * (2 * count))


def reduced_over_cores(keep, got, anchor, start):
    rows, part = keep.shape[1:]

    def kernel(keep_ref, got_ref, anchor_ref, send_ref, base_ref, held, sem):
        mine = bit_of(lax.axis_index("node"), 1)
        copy = pltpu.make_async_copy(anchor_ref.at[:, pl.ds(start, part)], held, sem)
        copy.start()

        def for_other(row):
            group = pl.ds(row, 16)
            send_ref[group] = narrow(wide(keep_ref[1 - mine, group]) + wide(got_ref[1 - mine, group]))

        by_rows(rows, for_other)
        copy.wait()

        def for_own(row):
            group = pl.ds(row, 16)
            total = wide(keep_ref[mine, group]) + wide(got_ref[mine, group])
            base_ref[group] = held[group] - base_rate * total

        by_rows(rows, for_own)

    return small_kernel(
        kernel,
        (keep, got, anchor),
        [in_vmem, in_vmem, any_place],
        [jax.ShapeDtypeStruct((rows, part), jnp.bfloat16), jax.ShapeDtypeStruct((rows, part), jnp.float32)],
        [in_vmem, in_vmem],
        [pltpu.VMEM((rows, part), jnp.float32), pltpu.SemaphoreType.DMA],
    )


def met(block, got, factor, gain, in_half, out_half):
    rows, part = got.shape
    sent = rows if out_half is None else rows // 2

    def kernel(block_ref, got_ref, send_ref, sum_ref):
        host = lax.axis_index("hst")
        first = 0 if in_half is None else bit_of(host, in_half) * rows

        def add(row):
            group = pl.ds(row, 16)
            total = block_ref[pl.ds(pl.multiple_of(first + row, 16), 16)] + factor * wide(got_ref[group])
            total = gain * total
            sum_ref[group] = total
            if out_half is None:
                send_ref[group] = narrow(total)

        by_rows(rows, add)
        if out_half is not None:
            other = (1 - bit_of(host, out_half)) * sent

            def give(row):
                send_ref[pl.ds(row, 16)] = narrow(sum_ref[pl.ds(pl.multiple_of(other + row, 16), 16)])

            by_rows(sent, give)

    return small_kernel(
        kernel,
        (block, got),
        [in_vmem, in_vmem],
        [jax.ShapeDtypeStruct((sent, part), jnp.bfloat16), jax.ShapeDtypeStruct((rows, part), jnp.float32)],
        [in_vmem, in_vmem],
    )


def finished(block, got, gain, half, anchor, momentum, momentum_out, start):
    rows = anchor.shape[0]
    part = block.shape[1]
    columns = pl.ds(start, part)

    def kernel(block_ref, got_ref, anchor_ref, momentum_ref, *rest):
        out_ref, fresh_ref, held_anchor, held_momentum, sems = rest[-5:]
        reads = [
            pltpu.make_async_copy(anchor_ref.at[:, columns], held_anchor, sems.at[0]),
            pltpu.make_async_copy(momentum_ref.at[:, columns], held_momentum, sems.at[1]),
        ]
        for read in reads:
            read.start()
        for read in reads:
            read.wait()

        def put(group, averaged):
            old, slow = held_anchor[group], held_momentum[group]
            fresh_ref[group] = narrow(
                (1.0 - slow_rate) * old + slow_rate * averaged - slow_rate * base_rate * slow_beta * slow
            )
            held_momentum[group] = slow_beta * slow + (old - averaged) * (1.0 / base_rate)

        if half is None:
            by_rows(rows, lambda row: put(pl.ds(row, 16), gain * (block_ref[pl.ds(row, 16)] + wide(got_ref[pl.ds(row, 16)]))))
        else:
            count = rows // 2
            mine = bit_of(lax.axis_index("hst"), half) * count
            own, other = mine, count - mine
            by_rows(count, lambda row: put(pl.ds(pl.multiple_of(own + row, 16), 16), block_ref[pl.ds(row, 16)]))
            by_rows(count, lambda row: put(pl.ds(pl.multiple_of(other + row, 16), 16), wide(got_ref[pl.ds(row, 16)])))
        write = pltpu.make_async_copy(held_momentum, out_ref.at[:, columns], sems.at[0])
        write.start()
        write.wait()

    held = [] if momentum_out is None else [momentum_out]
    momentum_out, fresh = small_kernel(
        kernel,
        (block, got, anchor, momentum, *held),
        [in_vmem, in_vmem, any_place, any_place] + [in_hbm] * len(held),
        [jax.ShapeDtypeStruct(anchor.shape, jnp.float32), jax.ShapeDtypeStruct((rows, part), jnp.bfloat16)],
        [in_hbm, in_vmem],
        [pltpu.VMEM((rows, part), jnp.float32)] * 2 + [pltpu.SemaphoreType.DMA((2,))],
        {4: 0} if held else None,
    )
    return fresh, momentum_out


def placed_in(weights, shape, pieces):
    blocks = [block for block, _, _ in pieces]

    def kernel(*refs):
        out_ref, sems = refs[-2:]
        node = lax.axis_index("node")
        copies = [
            pltpu.make_async_copy(
                refs[i], out_ref.at[jnp.bitwise_xor(node, flip), :, pl.ds(start, block.shape[1])], sems.at[i]
            )
            for i, (block, flip, start) in enumerate(pieces)
        ]
        for copy in copies:
            copy.start()
        for copy in copies:
            copy.wait()

    held = [] if weights is None else [weights]
    return small_kernel(
        kernel,
        (*blocks, *held),
        [in_vmem] * len(blocks) + [in_hbm] * len(held),
        [jax.ShapeDtypeStruct(shape, jnp.bfloat16)],
        [in_hbm],
        [pltpu.SemaphoreType.DMA((len(blocks),))],
        {len(blocks): 0} if held else None,
    )[0]


def chunk_steps(plan, sends, k, base, start, shared):
    (got,) = yield [(sends[k], "node", 1)]
    block, factor, in_half = base, -base_rate, None
    halved = []
    gain = 1.0 / (1 << len(plan))
    for place, (bit, by_halves) in enumerate(plan):
        send, block = met(block, got, factor, 1.0, in_half, bit if by_halves else None)
        (got,) = yield [(send, "hst", bit)]
        factor, in_half = 1.0, bit if by_halves else None
        halved += [bit] * by_halves
    half = None
    if halved:
        (half,) = halved
        send, block = met(block, got, factor, gain, in_half, None)
        shared["near"] = True
        (got,) = yield [(send, "hst", half)]
    fresh, shared["momentum"] = finished(
        block, got, gain, half, shared["anchor"], shared["momentum_in"], shared["momentum"], start
    )
    over_y, over_core = yield [(fresh, "node", 1), (fresh, "node", 0)]
    pieces = [(fresh, 0, start), (over_core, 1, start), (over_y, 2, start), *shared["late"]]
    shared["late"] = [(swapped(over_y, "node", 0), 3, start)]
    shared["weights"] = placed_in(shared["weights"], shared["shape"], pieces)


def update(plan, bounds, anchor, momentum, *sends_and_bases):
    rows, width = anchor.shape
    node_count = lax.axis_size("node")
    shared = {
        "anchor": anchor, "momentum_in": momentum, "momentum": None, "weights": None, "late": [],
        "shape": (node_count, rows, width),
    }
    sends, bases = list(sends_and_bases[0::2]), sends_and_bases[1::2]
    chunks = [chunk_steps(plan, sends, k, bases[k], bounds[k], shared) for k in range(len(bases))]
    arrived = [None] * len(chunks)
    last = None
    waiting = list(range(len(chunks)))
    waiting, later = waiting[:2], waiting[2:]
    steps = [0] * len(chunks)
    while waiting:
        k = waiting.pop(0)
        if arrived[k] is not None:
            held = {name: shared[name] for name in ("weights", "momentum") if shared[name] is not None}
            arrived[k], last, held = lax.optimization_barrier((arrived[k], last, held))
            shared.update(held)
        elif last is not None:
            sends[k], last = lax.optimization_barrier((sends[k], last))
        try:
            moves = chunks[k].send(arrived[k])
            last = [a for a, *_ in moves]
            arrived[k] = [swapped(*move) for move in moves]
            waiting.insert(1 if shared.pop("near", False) else len(waiting), k)
            if steps[k] == 1 and later:
                waiting.insert(0, later.pop(0))
            steps[k] += 1
        except StopIteration:
            pass
    weights = placed_in(shared["weights"], shared["shape"], shared["late"])
    return weights.reshape(-1, width), shared["momentum"]


def plan_of(bits):
    dear = len(bits) > 1 and bits[-1] > 1
    return [(bit, dear and bit == bits[0]) for bit in bits]


def local(hidden, cotangent, anchor, momentum, round_mask):
    hidden, cotangent, anchor, momentum = hidden[0], cotangent[0], anchor[0], momentum[0]
    tokens, width = cotangent.shape
    node_count, host_count = lax.axis_size("node"), lax.axis_size("hst")
    scale = 1.0 / (tokens * node_count)
    unit = width // chunk_count
    bounds = [unit * k for k in range(chunk_count + 1)]
    middle = chunk_count // 2

    def product(columns):
        left, right = hidden, cotangent[:, columns]
        whole = lax.dot_general(left, right, (((0,), (0,)), ((), ())), preferred_element_type=jnp.float32)
        return narrow(whole * scale)

    first = split_by_core(product(slice(0, bounds[middle])), node_count, middle)
    first, hidden = lax.optimization_barrier((first, hidden))
    first_gots = [swapped(part, "node", 0) for part in first[0::2]]
    later = split_by_core(product(slice(bounds[middle], width)), node_count, chunk_count - middle)
    first_gots, later_sends = lax.optimization_barrier((first_gots, later[0::2]))
    gots = [*first_gots, *(swapped(part, "node", 0) for part in later_sends)]
    handed = []
    for keep, got, start in zip([*first[1::2], *later[1::2]], gots, bounds):
        handed += reduced_over_cores(keep, got, anchor, start)
    branches = []
    for mask in range(1, host_count):
        bits = [b for b in range(host_count.bit_length() - 1) if mask >> b & 1]
        branches.append(lambda *arrays, plan=plan_of(bits): update(plan, bounds, *arrays))
    weights, momentum_new = lax.switch(
        round_mask[0] - 1, branches, anchor, momentum, *handed
    )
    return (weights[None], momentum_new[None])


def solution(mesh):
    placed = (
        P("hst", "node", None),
        P("hst", "node", None),
        P("hst", "node", None),
        P("hst", "node", None),
        P(),
    )
    return jax.shard_map(
        local,
        mesh=mesh,
        in_specs=placed,
        out_specs=(P("hst", None, None), P("hst", "node", None)),
        check_vma=False,
    )
```

```python
import jax
import jax.numpy as jnp
from jax import lax
from jax.experimental import pallas as pl
from jax.experimental.pallas import tpu as pltpu
from jax.sharding import PartitionSpec as P

base_rate = 0.5
slow_rate = 1.0
slow_beta = 0.7
chunk_count = 4


def swapped(block, axis, bit):
    count = lax.axis_size(axis)
    return lax.ppermute(block, axis, [(i, i ^ (1 << bit)) for i in range(count)])


def bit_of(index, bit):
    return jnp.bitwise_and(jnp.right_shift(index, bit), 1)


def wide(block):
    return block.astype(jnp.float32)


def narrow(block):
    return block.astype(jnp.bfloat16)


any_place = pl.BlockSpec(memory_space=pl.ANY)
in_hbm = pl.BlockSpec(memory_space=pltpu.HBM)
in_vmem = pl.BlockSpec(memory_space=pltpu.VMEM)


def small_kernel(body, ins, in_specs, outs, out_specs, scratch=(), aliases=None):
    return pl.pallas_call(
        body,
        out_shape=outs,
        in_specs=in_specs,
        out_specs=out_specs,
        scratch_shapes=list(scratch),
        input_output_aliases=aliases or {},
        compiler_params=pltpu.CompilerParams(vmem_limit_bytes=12 * 2**20),
        cost_estimate=pl.CostEstimate(flops=1024, bytes_accessed=1024, transcendentals=0),
    )(*ins)


def by_rows(count, step):
    @pl.loop(0, count // 16)
    def _(group):
        step(pl.multiple_of(group * 16, 16))


def split_by_core(product, node_count, count):
    rows, part = product.shape[0] // node_count, product.shape[1] // count

    def kernel(product_ref, *outs):
        core = bit_of(lax.axis_index("node"), 0)
        for chunk in range(count):
            for pair in range(node_count // 2):
                for out_ref, first in zip(outs[2 * chunk : 2 * chunk + 2], (1 - core, core)):

                    def move(row, out_ref=out_ref, first=first, chunk=chunk, pair=pair):
                        source = pl.ds(pl.multiple_of((2 * pair + first) * rows + row, 16), 16)
                        out_ref[pair, pl.ds(row, 16)] = product_ref[source, chunk * part : (chunk + 1) * part]

                    by_rows(rows, move)

    half = jax.ShapeDtypeStruct((node_count // 2, rows, part), jnp.bfloat16)
    return small_kernel(kernel, (product,), [in_vmem], [half] * (2 * count), [in_vmem] * (2 * count))


def reduced_over_cores(keep, got, anchor, start):
    rows, part = keep.shape[1:]

    def kernel(keep_ref, got_ref, anchor_ref, send_ref, base_ref, held, sem):
        mine = bit_of(lax.axis_index("node"), 1)
        copy = pltpu.make_async_copy(anchor_ref.at[:, pl.ds(start, part)], held, sem)
        copy.start()

        def for_other(row):
            group = pl.ds(row, 16)
            send_ref[group] = narrow(wide(keep_ref[1 - mine, group]) + wide(got_ref[1 - mine, group]))

        by_rows(rows, for_other)
        copy.wait()

        def for_own(row):
            group = pl.ds(row, 16)
            total = wide(keep_ref[mine, group]) + wide(got_ref[mine, group])
            base_ref[group] = held[group] - base_rate * total

        by_rows(rows, for_own)

    return small_kernel(
        kernel,
        (keep, got, anchor),
        [in_vmem, in_vmem, any_place],
        [jax.ShapeDtypeStruct((rows, part), jnp.bfloat16), jax.ShapeDtypeStruct((rows, part), jnp.float32)],
        [in_vmem, in_vmem],
        [pltpu.VMEM((rows, part), jnp.float32), pltpu.SemaphoreType.DMA],
    )


def met(block, got, factor, gain, in_half, out_half):
    rows, part = got.shape
    sent = rows if out_half is None else rows // 2

    def kernel(block_ref, got_ref, send_ref, sum_ref):
        host = lax.axis_index("hst")
        first = 0 if in_half is None else bit_of(host, in_half) * rows

        def add(row):
            group = pl.ds(row, 16)
            total = block_ref[pl.ds(pl.multiple_of(first + row, 16), 16)] + factor * wide(got_ref[group])
            total = gain * total
            sum_ref[group] = total
            if out_half is None:
                send_ref[group] = narrow(total)

        by_rows(rows, add)
        if out_half is not None:
            other = (1 - bit_of(host, out_half)) * sent

            def give(row):
                send_ref[pl.ds(row, 16)] = narrow(sum_ref[pl.ds(pl.multiple_of(other + row, 16), 16)])

            by_rows(sent, give)

    return small_kernel(
        kernel,
        (block, got),
        [in_vmem, in_vmem],
        [jax.ShapeDtypeStruct((sent, part), jnp.bfloat16), jax.ShapeDtypeStruct((rows, part), jnp.float32)],
        [in_vmem, in_vmem],
    )


def finished(block, got, gain, half, anchor, momentum, momentum_out, start):
    rows = anchor.shape[0]
    part = block.shape[1]
    columns = pl.ds(start, part)

    def kernel(block_ref, got_ref, anchor_ref, momentum_ref, *rest):
        out_ref, fresh_ref, held_anchor, held_momentum, sems = rest[-5:]
        reads = [
            pltpu.make_async_copy(anchor_ref.at[:, columns], held_anchor, sems.at[0]),
            pltpu.make_async_copy(momentum_ref.at[:, columns], held_momentum, sems.at[1]),
        ]
        for read in reads:
            read.start()
        for read in reads:
            read.wait()

        def put(group, averaged):
            old, slow = held_anchor[group], held_momentum[group]
            fresh_ref[group] = narrow(
                (1.0 - slow_rate) * old + slow_rate * averaged - slow_rate * base_rate * slow_beta * slow
            )
            held_momentum[group] = slow_beta * slow + (old - averaged) * (1.0 / base_rate)

        if half is None:
            by_rows(rows, lambda row: put(pl.ds(row, 16), gain * (block_ref[pl.ds(row, 16)] + wide(got_ref[pl.ds(row, 16)]))))
        else:
            count = rows // 2
            mine = bit_of(lax.axis_index("hst"), half) * count
            own, other = mine, count - mine
            by_rows(count, lambda row: put(pl.ds(pl.multiple_of(own + row, 16), 16), block_ref[pl.ds(row, 16)]))
            by_rows(count, lambda row: put(pl.ds(pl.multiple_of(other + row, 16), 16), wide(got_ref[pl.ds(row, 16)])))
        write = pltpu.make_async_copy(held_momentum, out_ref.at[:, columns], sems.at[0])
        write.start()
        write.wait()

    held = [] if momentum_out is None else [momentum_out]
    momentum_out, fresh = small_kernel(
        kernel,
        (block, got, anchor, momentum, *held),
        [in_vmem, in_vmem, any_place, any_place] + [in_hbm] * len(held),
        [jax.ShapeDtypeStruct(anchor.shape, jnp.float32), jax.ShapeDtypeStruct((rows, part), jnp.bfloat16)],
        [in_hbm, in_vmem],
        [pltpu.VMEM((rows, part), jnp.float32)] * 2 + [pltpu.SemaphoreType.DMA((2,))],
        {4: 0} if held else None,
    )
    return fresh, momentum_out


def placed_in(weights, shape, pieces):
    blocks = [block for block, _, _ in pieces]

    def kernel(*refs):
        out_ref, sems = refs[-2:]
        node = lax.axis_index("node")
        copies = [
            pltpu.make_async_copy(
                refs[i], out_ref.at[jnp.bitwise_xor(node, flip), :, pl.ds(start, block.shape[1])], sems.at[i]
            )
            for i, (block, flip, start) in enumerate(pieces)
        ]
        for copy in copies:
            copy.start()
        for copy in copies:
            copy.wait()

    held = [] if weights is None else [weights]
    return small_kernel(
        kernel,
        (*blocks, *held),
        [in_vmem] * len(blocks) + [in_hbm] * len(held),
        [jax.ShapeDtypeStruct(shape, jnp.bfloat16)],
        [in_hbm],
        [pltpu.SemaphoreType.DMA((len(blocks),))],
        {len(blocks): 0} if held else None,
    )[0]


def chunk_steps(plan, sends, k, base, start, shared):
    (got,) = yield [(sends[k], "node", 1)]
    block, factor, in_half = base, -base_rate, None
    halved = []
    gain = 1.0 / (1 << len(plan))
    for place, (bit, by_halves) in enumerate(plan):
        send, block = met(block, got, factor, 1.0, in_half, bit if by_halves else None)
        (got,) = yield [(send, "hst", bit)]
        factor, in_half = 1.0, bit if by_halves else None
        halved += [bit] * by_halves
    half = None
    if halved:
        (half,) = halved
        send, block = met(block, got, factor, gain, in_half, None)
        shared["near"] = len(plan) == 2
        (got,) = yield [(send, "hst", half)]
    fresh, shared["momentum"] = finished(
        block, got, gain, half, shared["anchor"], shared["momentum_in"], shared["momentum"], start
    )
    over_y, over_core = yield [(fresh, "node", 1), (fresh, "node", 0)]
    pieces = [(fresh, 0, start), (over_core, 1, start), (over_y, 2, start), *shared["late"]]
    shared["late"] = [(swapped(over_y, "node", 0), 3, start)]
    shared["weights"] = placed_in(shared["weights"], shared["shape"], pieces)


def update(plan, bounds, anchor, momentum, *sends_and_bases):
    rows, width = anchor.shape
    node_count = lax.axis_size("node")
    shared = {
        "anchor": anchor, "momentum_in": momentum, "momentum": None, "weights": None, "late": [],
        "shape": (node_count, rows, width),
    }
    sends, bases = list(sends_and_bases[0::2]), sends_and_bases[1::2]
    chunks = [chunk_steps(plan, sends, k, bases[k], bounds[k], shared) for k in range(len(bases))]
    arrived = [None] * len(chunks)
    last = None
    waiting = list(range(len(chunks)))
    waiting, later = waiting[:2], waiting[2:]
    steps = [0] * len(chunks)
    while waiting:
        k = waiting.pop(0)
        if arrived[k] is not None:
            held = {name: shared[name] for name in ("weights", "momentum") if shared[name] is not None}
            arrived[k], last, held = lax.optimization_barrier((arrived[k], last, held))
            shared.update(held)
        elif last is not None:
            sends[k], last = lax.optimization_barrier((sends[k], last))
        try:
            moves = chunks[k].send(arrived[k])
            last = [a for a, *_ in moves]
            arrived[k] = [swapped(*move) for move in moves]
            waiting.insert(1 if shared.pop("near", False) else len(waiting), k)
            if steps[k] == 1 and later:
                waiting.insert(0, later.pop(0))
            steps[k] += 1
        except StopIteration:
            pass
    weights = placed_in(shared["weights"], shared["shape"], shared["late"])
    return weights.reshape(-1, width), shared["momentum"]


def plan_of(bits):
    dear = len(bits) > 1 and bits[-1] > 1
    return [(bit, dear and bit == bits[-2]) for bit in bits]


def local(hidden, cotangent, anchor, momentum, round_mask):
    hidden, cotangent, anchor, momentum = hidden[0], cotangent[0], anchor[0], momentum[0]
    tokens, width = cotangent.shape
    node_count, host_count = lax.axis_size("node"), lax.axis_size("hst")
    scale = 1.0 / (tokens * node_count)
    unit = width // chunk_count
    bounds = [unit * k for k in range(chunk_count + 1)]
    middle = chunk_count // 2

    def product(columns):
        left, right = hidden, cotangent[:, columns]
        whole = lax.dot_general(left, right, (((0,), (0,)), ((), ())), preferred_element_type=jnp.float32)
        return narrow(whole * scale)

    first = split_by_core(product(slice(0, bounds[middle])), node_count, middle)
    first, hidden = lax.optimization_barrier((first, hidden))
    first_gots = [swapped(part, "node", 0) for part in first[0::2]]
    later = split_by_core(product(slice(bounds[middle], width)), node_count, chunk_count - middle)
    first_gots, later_sends = lax.optimization_barrier((first_gots, later[0::2]))
    gots = [*first_gots, *(swapped(part, "node", 0) for part in later_sends)]
    handed = []
    for keep, got, start in zip([*first[1::2], *later[1::2]], gots, bounds):
        handed += reduced_over_cores(keep, got, anchor, start)
    branches = []
    for mask in range(1, host_count):
        bits = [b for b in range(host_count.bit_length() - 1) if mask >> b & 1]
        branches.append(lambda *arrays, plan=plan_of(bits): update(plan, bounds, *arrays))
    weights, momentum_new = lax.switch(
        round_mask[0] - 1, branches, anchor, momentum, *handed
    )
    return (weights[None], momentum_new[None])


def solution(mesh):
    placed = (
        P("hst", "node", None),
        P("hst", "node", None),
        P("hst", "node", None),
        P("hst", "node", None),
        P(),
    )
    return jax.shard_map(
        local,
        mesh=mesh,
        in_specs=placed,
        out_specs=(P("hst", None, None), P("hst", "node", None)),
        check_vma=False,
    )
```
